128 devices in a mesh: grp: 4 (over x), blk: 32 (over y, z, core).
Axes of the slice: x: 4, y: 4, z: 4, core: 2. Of those that a mesh axis runs over, the one named last changes fastest.
Arguments:
- t2_tiles: bfloat16 [1024, 64, 2304], P(('grp', 'blk')), may hold values from -6 to 6
- t2_shape: int32 [1024, 1], P(('grp', 'blk')), may hold values 0 or 1
- owners: int32 [1024, 1], P(('grp', 'blk')), may hold values from 0 to 3; in each aligned block of 8 rows (0 to 7, 8 to 15, ...) at most 4 rows name the same one
- integrals: bfloat16 [2304, 2304], P('blk'), may hold values from -0.125 to 0.125
Outputs:
- residual: bfloat16 [2048, 64, 2304], P(('grp', 'blk'))
The draws below stay inside these ranges and needn't reach their ends.
Inputs may be any that keep to these rules, and one draw needn't show every extreme that they name: `owners`: among the 8 tiles of one device, no group is named more than 4 times, a bound that some block reaches.
All inputs are finite; a program needn't handle non-finite values. No bound on the sum of `t2_shape` on one device may be relied on, other than what follows from the above.
Results may differ from the reference program's by a relative error of at most 0.001.
Values may be sent and summed in bfloat16 or wider, within the bound.
No kernel may reach another device: no remote copies, remote signals or barrier semaphores. Data moves between devices by JAX's collectives and lax.ppermute only.
A program may use at most 64 MiB of HBM per device.

```python
import math
import jax
import jax.numpy as jnp
import numpy as np
from jax import lax

PW = 2304
OW = 64
NOT_DEV = 8
CAP = 4
NOT = 1024
RT = 2048
N_GRP = 4
N_BLK = 32


def plant(values, key, low, top_value):
    dims = values.shape
    spot = [jax.random.randint(jax.random.fold_in(key, axis), (), 0, dims[axis]) for axis in range(len(dims))]
    values = values.at[tuple(spot)].set(low)
    longest = dims.index(max(dims))
    spot[longest] = (spot[longest] + 1) % dims[longest]
    return values.at[tuple(spot)].set(top_value)


def levels(stream_key, extent, cuts, smallest, top_value):
    gain, own = 1.0, jax.random.fold_in(stream_key, 6)
    for dim, blocks in cuts:
        heights = jnp.exp(jax.random.uniform(jax.random.fold_in(own, dim), (blocks,), jnp.float32, smallest / len(cuts), top_value / len(cuts)))
        gain = gain * jnp.repeat(heights, extent[dim] // blocks).reshape([-1 if axis == dim else 1 for axis in range(len(extent))])
    return gain


def deal_out(stream_key, own, number, rows, number_of, top, bound, slope):
    ranking = jax.random.permutation(stream_key, number_of)
    crowded, common = shares(number_of, rows * top, bound, slope, True), shares(number_of, rows * top, bound, slope, False)
    places = jnp.arange(number_of)

    def named(sizes, offset_by):
        used = int((sizes > 0).sum())
        fixed = max(1, used // 4)
        shifted = fixed + (places - fixed + offset_by * (used - fixed)) % max(1, number_of - fixed)
        return jnp.zeros((number_of,), jnp.int32).at[ranking[jnp.where(places < fixed, places, shifted)]].set(jnp.asarray(sizes, jnp.int32))

    sizes = jnp.where(number % 4 == 0, named(crowded, number // 4), named(common, number - number // 4 - 1))
    mixed = jax.random.permutation(jax.random.fold_in(own, 3), number_of)
    giver, taker = mixed[0:number_of // 2 * 2:2], mixed[1:number_of // 2 * 2:2]
    room = jnp.minimum(sizes[giver] - 1, bound - sizes[taker]) // 2
    room = jnp.where((giver == ranking[0]) | (taker == ranking[0]) | (sizes[taker] == 0), 0, jnp.maximum(room, 0))
    shifted = jax.random.randint(jax.random.fold_in(own, 4), (number_of // 2,), 0, 1 << 20) % (room + 1)
    sizes = sizes.at[giver].add(-shifted).at[taker].add(shifted)
    labels = jnp.searchsorted(jnp.cumsum(sizes), jnp.arange(rows * top), side="right").astype(jnp.int32)
    table = labels.reshape(top, rows).T
    table = table[jax.random.permutation(jax.random.fold_in(own, 1), rows)]
    offset_by = jax.random.randint(jax.random.fold_in(own, 2), (rows, 1), 0, top)
    return jnp.take_along_axis(table, (jnp.arange(top)[None, :] + offset_by) % top, axis=1)


def shares(count, total, most, lean, full):
    portions = [(1 << 20) // math.isqrt(standing ** lean) + 1 for standing in range(1, count + 1)]
    largest = most if full else min(most, max(-(-total // count), total * portions[0] // sum(portions)))
    least = 1 if total - largest >= count - 1 else 0
    given, surplus = [largest] + [least] * (count - 1), total - largest - least * (count - 1)
    while surplus > 0:
        movable = [i for i in range(1, count) if given[i] < largest] or [i for i in range(1, count) if given[i] < most]
        whole, left = sum([portions[i] for i in movable]), surplus
        for i in movable:
            addition = min(most - given[i], max(1, left * portions[i] // whole), surplus)
            given[i] = given[i] + addition
            surplus = surplus - addition
    return np.array(given)


def normal_values(stream_key, shape, deviation, most, split=(), kind=jnp.bfloat16):
    loudness = levels(stream_key, shape, split, -0.22, 0.18) if split else 1.0
    array = jax.random.normal(stream_key, shape, jnp.float32) * deviation * loudness
    return jnp.minimum(jnp.maximum(array, -most), most).astype(kind)


def setup_inputs(seed: int = 0) -> dict:
    key_list = jax.random.split(jax.random.key(seed), 5)
    t2_tiles = normal_values(key_list[0], (NOT, OW, PW), 1.0, 6.0, ((0, 128),))
    t2_shape = plant((jax.random.randint(key_list[1], (NOT, 1), 0, 4) < 3).astype(jnp.int32), jax.random.fold_in(key_list[1], 1), 0, 1)
    owners_keys = jax.random.split(jax.random.fold_in(key_list[2], 1), NOT // NOT_DEV)
    owners_turns = jax.random.permutation(jax.random.fold_in(key_list[2], 3), NOT // NOT_DEV)
    owners = jax.vmap(lambda own, number: deal_out(jax.random.fold_in(key_list[2], 2), own, number, NOT_DEV, N_GRP, 1, CAP, 2))(owners_keys, owners_turns).reshape((NOT, 1))
    integrals = normal_values(key_list[3], (PW, PW), PW ** -0.5, 0.125, ((0, 32),))
    return dict(t2_tiles=t2_tiles, t2_shape=t2_shape, owners=owners, integrals=integrals)


def reference(t2_tiles, t2_shape, owners, integrals):
    devices = N_GRP * N_BLK
    tiles = t2_tiles.reshape(devices, NOT_DEV, OW, PW)
    keep = t2_shape.reshape(devices, NOT_DEV)
    owned = owners.reshape(devices, NOT_DEV).astype(jnp.int32)
    position = jnp.arange(NOT_DEV, dtype=jnp.int32)
    earlier = (owned[:, None, :] == owned[:, :, None]) & (position[None, None, :] < position[None, :, None])
    rank = jnp.sum(earlier.astype(jnp.int32), axis=2).astype(jnp.int32)
    device = jnp.arange(devices, dtype=jnp.int32)
    group = device // N_BLK
    column = device % N_BLK
    target = (owned * N_BLK + column[:, None]) * (N_GRP * CAP) + group[:, None] * CAP + rank
    target = target.astype(jnp.int32)

    def one_block(pair):
        block, flags = pair
        masked = jnp.where(flags[:, None, None] > 0, block, jnp.zeros_like(block))
        rows = masked.reshape(NOT_DEV * OW, PW)
        product = jnp.dot(rows, integrals.T, preferred_element_type=jnp.float32)
        return product.astype(jnp.bfloat16).reshape(NOT_DEV, OW, PW)

    results = lax.map(one_block, (tiles, keep))
    flat = results.reshape(devices * NOT_DEV, OW, PW)
    residual = jnp.zeros((RT, OW, PW), t2_tiles.dtype)
    return residual.at[target.reshape(-1)].set(flat)
```

```python
import functools

import jax
import jax.numpy as jnp
from jax import lax
from jax.experimental import pallas as pl
from jax.experimental.pallas import tpu as pltpu
from jax.sharding import PartitionSpec as P

Y = 4
CAP = 4
MARK = 16
ANY = pl.BlockSpec(memory_space=pl.ANY)
SMEM = pl.BlockSpec(memory_space=pltpu.SMEM)
VMEM = pl.BlockSpec(memory_space=pltpu.VMEM)
BF16 = jnp.bfloat16


def pack_kernel(split, owners, shape, t2, code, *refs):
    outs, sem = refs[:-1], refs[-1]
    for out, size in zip(outs, split, strict=True):
        for h in range(4):
            for k in range(size):
                out[h, k, :MARK, :128] = jnp.full((MARK, 128), jnp.nan, out.dtype)
    for t in range(8):
        rank = 0
        for e in range(t):
            rank = rank + (owners[e] == owners[t]).astype(jnp.int32)
        code[t] = owners[t] + 4 * rank + 16 * (shape[t] > 0).astype(jnp.int32)

    def each(do):
        for t in range(8):
            owner, rank = lax.bitwise_and(code[t], 3), lax.bitwise_and(lax.shift_right_logical(code[t], 2), 3)
            first = 0
            for out, size in zip(outs, split, strict=True):

                @pl.when((code[t] >= 16) & (rank >= first) & (rank < first + size))
                def _():
                    do(pltpu.make_async_copy(t2.at[t], out.at[owner, jnp.clip(rank - first, 0, size - 1)], sem.at[t]))

                first += size

    each(lambda c: c.start())
    each(lambda c: c.wait())


def pack(owners, shape, t2, split):
    bufs = tuple(jax.ShapeDtypeStruct((4, n) + t2.shape[1:], t2.dtype) for n in split)
    return pl.pallas_call(
        functools.partial(pack_kernel, split),
        out_shape=(jax.ShapeDtypeStruct((8,), jnp.int32),) + bufs,
        in_specs=[SMEM, SMEM, ANY],
        out_specs=(SMEM,) + (VMEM,) * len(bufs),
        scratch_shapes=[pltpu.SemaphoreType.DMA((8,))],
        compiler_params=pltpu.CompilerParams(vmem_limit_bytes=32 << 20),
        cost_estimate=pl.CostEstimate(flops=0, bytes_accessed=4_700_000, transcendentals=0),
    )(owners, shape, t2)


def pieces_of(y, z, c):
    a, b = jnp.where(c == 0, y, z), jnp.where(c == 0, z, y)

    def chip(da, db):
        aa, bb = lax.bitwise_and(a + da, 3), lax.bitwise_and(b + db, 3)
        return jnp.where(c == 0, aa * Y + bb, bb * Y + aa)

    near = lambda db: [chip(0, db), chip(-1, db)]
    wide = lambda db: [chip(1, db), chip(2, db)]
    return near(0) + wide(0) + near(-1) + wide(1) + wide(-1) + near(1) + near(2) + wide(2)


def product_kernel(split, counts, position, code, local, *refs):
    arrived, refs = refs[: len(split)], refs[len(split) :]
    mine, refs = refs[: counts[0]], refs[counts[0] :]
    sibling, refs = refs[: counts[1]], refs[counts[1] :]
    out, rows, matrix, result, zero, marks, slots, source, sem_t, sem_i, sem_o, sem_z, sem_m = refs
    half = matrix.shape[1] // 2
    y, z, c, g = position[0], position[1], position[2], position[3]

    copies = []
    for side, buffers in enumerate((mine, sibling)):
        core = c if side == 0 else 1 - c
        sources_of = []
        for buffer in buffers:
            sources_of += [buffer] if len(buffer.shape) == 2 else [buffer.at[k] for k in range(buffer.shape[0])]
        for n, (piece, chip) in enumerate(zip(sources_of, pieces_of(y, z, core), strict=True)):
            height = piece.shape[0]
            to = matrix.at[pl.ds(pl.multiple_of(chip * height, height), height), pl.ds(pl.multiple_of(core * half, 128), half)]
            copies.append(pltpu.make_async_copy(piece, to, sem_i.at[side, n]))
    for copy in copies:
        copy.start()

    looks = []
    for buffer, size in zip(arrived, split, strict=True):
        at = len(looks) // 4
        for h in range(4):
            for k in range(size):
                slot = h * CAP + at + k
                looks.append(pltpu.make_async_copy(buffer.at[h, k, pl.ds(0, MARK), pl.ds(0, 128)], marks.at[slot], sem_m.at[slot]))
    for look in looks:
        look.start()
    for look in looks:
        look.wait()
    for s in range(16):
        found = jnp.max(jnp.where(jnp.isnan(marks[s].astype(jnp.float32)), 0.0, 1.0)) > 0.5
        source[s] = jnp.where(found & (g != s // CAP), 0, -1)
    for t in range(8):
        rank = lax.bitwise_and(lax.shift_right_logical(code[t], 2), 3)

        @pl.when((code[t] >= 16) & (lax.bitwise_and(code[t], 3) == g))
        def _():
            source[g * CAP + rank] = t

    zero[...] = jnp.zeros_like(zero)
    count = jnp.int32(0)
    for s in range(16):
        taken = source[s] >= 0
        own = g == s // CAP
        first = 0

        @pl.when(taken & own)
        def _():
            pltpu.make_async_copy(local.at[jnp.maximum(source[s], 0)], rows.at[count], sem_t.at[s]).start()

        for buffer, size in zip(arrived, split, strict=True):
            if first <= s % CAP < first + size:

                @pl.when(taken & jnp.logical_not(own))
                def _():
                    pltpu.make_async_copy(buffer.at[s // CAP, s % CAP - first], rows.at[count], sem_t.at[s]).start()

            first += size

        @pl.when(taken)
        def _():
            slots[count] = s

        @pl.when(jnp.logical_not(taken))
        def _():
            pltpu.make_async_copy(zero, out.at[s], sem_z.at[s]).start()

        count = count + taken.astype(jnp.int32)
    for s in range(16):

        @pl.when(source[s] >= 0)
        def _():
            pltpu.make_async_copy(local.at[0], rows.at[0], sem_t.at[s]).wait()

    for copy in copies:
        copy.wait()

    width = matrix.shape[0]
    step = 256
    occ = rows.shape[1]
    group = 4

    @pl.loop(0, lax.shift_right_logical(count + group - 1, 2))
    def _(m):
        left = rows[pl.ds(m * group, group)].reshape(group * occ, width)
        for n in range(width // step):
            right = matrix[n * step : (n + 1) * step, :]
            acc = lax.dot_general(left, right, (((1,), (1,)), ((), ())), preferred_element_type=jnp.float32)
            result[pl.ds(m * group, group), :, n * step : (n + 1) * step] = acc.astype(result.dtype).reshape(group, occ, step)
        for j in range(group):

            @pl.when(m * group + j < count)
            def _():
                pltpu.make_async_copy(result.at[m * group + j], out.at[slots[m * group + j]], sem_o.at[m * group + j]).start()

    for s in range(16):

        @pl.when(s < count)
        def _():
            pltpu.make_async_copy(result.at[s], out.at[slots[s]], sem_o.at[s]).wait()

        @pl.when(source[s] < 0)
        def _():
            pltpu.make_async_copy(zero, out.at[s], sem_z.at[s]).wait()


def product(position, code, local, arrived, mine, sibling):
    occ, width = local.shape[1:]
    split = tuple(a.shape[1] for a in arrived)
    return pl.pallas_call(
        functools.partial(product_kernel, split, (len(mine), len(sibling))),
        out_shape=jax.ShapeDtypeStruct((16, occ, width), BF16),
        in_specs=[SMEM, SMEM] + [ANY] * (1 + len(arrived) + len(mine) + len(sibling)),
        out_specs=ANY,
        scratch_shapes=[
            pltpu.VMEM((16, occ, width), BF16),
            pltpu.VMEM((width, width), BF16),
            pltpu.VMEM((16, occ, width), BF16),
            pltpu.VMEM((occ, width), BF16),
            pltpu.VMEM((16, MARK, 128), BF16),
            pltpu.SMEM((16,), jnp.int32),
            pltpu.SMEM((16,), jnp.int32),
            pltpu.SemaphoreType.DMA((16,)),
            pltpu.SemaphoreType.DMA((2, 16)),
            pltpu.SemaphoreType.DMA((16,)),
            pltpu.SemaphoreType.DMA((16,)),
            pltpu.SemaphoreType.DMA((16,)),
        ],
        compiler_params=pltpu.CompilerParams(vmem_limit_bytes=48 << 20),
        cost_estimate=pl.CostEstimate(flops=2 * 832 * width * width, bytes_accessed=20_000_000, transcendentals=0),
    )(position, code, local, *arrived, *mine, *sibling)


def index(y, z, c):
    return ((y % Y) * Y + z % Y) * 2 + c


def permutation(move):
    return [(index(y, z, c), index(*move(y, z, c))) for y in range(Y) for z in range(Y) for c in range(2)]


SWAP = permutation(lambda y, z, c: (y, z, 1 - c))


def first(s):
    return permutation(lambda y, z, c: (y + s, z, c) if c == 0 else (y, z + s, c))


def second(s):
    return permutation(lambda y, z, c: (y, z + s, c) if c == 0 else (y + s, z, c))


def send(x, pairs):
    return lax.ppermute(x, "blk", pairs)


def ring(x, s):
    return lax.ppermute(x, "grp", [(g, (g + s) % 4) for g in range(4)])


def rows_of_chip(integrals):
    core = lax.axis_index("blk") % 2
    half = integrals.shape[1] // 2
    sibling = send(integrals, SWAP)
    rows = jnp.concatenate([jnp.where(core == 0, integrals, sibling), jnp.where(core == 0, sibling, integrals)], 0)
    left, right = rows[:, :half], rows[:, half:]
    return jnp.where(core == 0, left, right), jnp.where(core == 0, right, left)


def gather(own, other):
    before, behind, opposite = send(own, first(1)), send(own, first(-1)), send(own, first(2))
    near, wide = jnp.stack([own, before]), jnp.stack([behind, opposite])
    near_up, wide_down = send(near, second(1)), send(wide, second(-1))
    wide_up, near_down = send(wide, second(1)), send(near, second(-1))
    near_far, wide_far = send(near_up, second(1)), send(wide_down, second(-1))
    moved = [near_up, wide_down, wide_up, near_down, near_far, wide_far]
    return [near, wide] + moved, [other, send(before, SWAP), send(wide, SWAP)] + [send(m, SWAP) for m in moved]


def as_one(owners, f, *args):
    empty = lambda *a: jax.tree.map(lambda x: jnp.zeros(x.shape, x.dtype), jax.eval_shape(f, *a))
    return lax.cond(owners[0, 0] >= 0, f, empty, *args)


SPLIT = (4,)


def body(t2, t2_shape, owners, integrals):
    g, b = lax.axis_index("grp"), lax.axis_index("blk")
    position = jnp.stack([b // 8, (b // 2) % 4, b % 2, g]).astype(jnp.int32)
    code, *out = pack(owners[:, 0], t2_shape[:, 0], t2, SPLIT)
    arrived = [lax.all_to_all(o, "grp", split_axis=0, concat_axis=0, tiled=True) for o in out]
    mine, sibling = as_one(owners, gather, *rows_of_chip(integrals))
    return product(position, code, t2, arrived, mine, sibling)


def solution(mesh):
    in_specs = (
        P(("grp", "blk"), None, None),
        P(("grp", "blk"), None),
        P(("grp", "blk"), None),
        P("blk", None),
    )
    out_specs = P(("grp", "blk"), None, None)
    return jax.shard_map(body, mesh=mesh, in_specs=in_specs, out_specs=out_specs, check_vma=False)
```

```python
import functools

import jax
import jax.numpy as jnp
from jax import lax
from jax.experimental import pallas as pl
from jax.experimental.pallas import tpu as pltpu
from jax.sharding import PartitionSpec as P

Y = 4
CAP = 4
MARK = 16
ANY = pl.BlockSpec(memory_space=pl.ANY)
SMEM = pl.BlockSpec(memory_space=pltpu.SMEM)
VMEM = pl.BlockSpec(memory_space=pltpu.VMEM)
BF16 = jnp.bfloat16


def pack_kernel(owners_hbm, shape_hbm, t2, code, out, owners, shape, tiles, mark, sem_s, sem_i, sem_o, sem_m):
    small = [pltpu.make_async_copy(owners_hbm, owners, sem_s.at[0]), pltpu.make_async_copy(shape_hbm, shape, sem_s.at[1])]
    for load in small:
        load.start()
    loads = [pltpu.make_async_copy(t2.at[t], tiles.at[t], sem_i.at[t]) for t in range(8)]
    for load in loads:
        load.start()
    mark[...] = jnp.full(mark.shape, jnp.nan, mark.dtype)
    for load in small:
        load.wait()
    taken = jnp.int32(0)
    for t in range(8):
        rank = 0
        for e in range(t):
            rank = rank + (owners[e] == owners[t]).astype(jnp.int32)
        live = (shape[t] > 0).astype(jnp.int32)
        code[t] = owners[t] + 4 * rank + 16 * live
        taken = taken | lax.shift_left(live, owners[t] * CAP + rank)

    def marks(do):
        for s in range(16):

            @pl.when(lax.bitwise_and(lax.shift_right_logical(taken, s), 1) == 0)
            def _():
                do(pltpu.make_async_copy(mark, out.at[s // CAP, s % CAP, pl.ds(0, MARK), pl.ds(0, 128)], sem_m.at[s]))

    def moves(do):
        for t in range(8):

            @pl.when(code[t] >= 16)
            def _():
                place = out.at[lax.bitwise_and(code[t], 3), lax.bitwise_and(lax.shift_right_logical(code[t], 2), 3)]
                do(loads[t], pltpu.make_async_copy(tiles.at[t], place, sem_o.at[t]))

            if do is start:

                @pl.when(code[t] < 16)
                def _():
                    loads[t].wait()

    def start(load, move):
        load.wait()
        move.start()

    marks(lambda c: c.start())
    moves(start)
    marks(lambda c: c.wait())
    moves(lambda load, move: move.wait())


def pack(owners, shape, t2):
    return pl.pallas_call(
        pack_kernel,
        out_shape=(jax.ShapeDtypeStruct((8,), jnp.int32), jax.ShapeDtypeStruct((4, CAP) + t2.shape[1:], t2.dtype)),
        in_specs=[ANY, ANY, ANY],
        out_specs=(SMEM, ANY),
        scratch_shapes=[
            pltpu.SMEM((8,), jnp.int32),
            pltpu.SMEM((8,), jnp.int32),
            pltpu.VMEM(t2.shape, t2.dtype),
            pltpu.VMEM((MARK, 128), t2.dtype),
            pltpu.SemaphoreType.DMA((2,)),
            pltpu.SemaphoreType.DMA((8,)),
            pltpu.SemaphoreType.DMA((8,)),
            pltpu.SemaphoreType.DMA((16,)),
        ],
        compiler_params=pltpu.CompilerParams(vmem_limit_bytes=56 << 20),
        cost_estimate=pl.CostEstimate(flops=0, bytes_accessed=4_700_000, transcendentals=0),
    )(owners, shape, t2)


def chips_of(y, z, c):
    a, b = jnp.where(c == 0, y, z), jnp.where(c == 0, z, y)

    def chip(da, db):
        aa, bb = lax.bitwise_and(a + da, 3), lax.bitwise_and(b + db, 3)
        return jnp.where(c == 0, aa * Y + bb, bb * Y + aa)

    near = lambda db: [chip(0, db), chip(-1, db)]
    wide = lambda db: [chip(1, db), chip(2, db)]
    return near(0) + wide(0) + near(-1) + wide(1) + wide(-1) + near(1) + near(2) + wide(2)


def product_kernel(place, code, local, arrived, *refs):
    mine, sibling, refs = refs[:8], refs[8:16], refs[16:]
    out, rows, matrix, result, zero, source, order, sem_t, sem_i, sem_o, sem_z = refs
    y, z, c, g = place[0], place[1], place[2], place[3]
    half = matrix.shape[1] // 2
    height = mine[0].shape[1]
    width = matrix.shape[0]
    step, occ = 256, rows.shape[1]

    for s in range(16):
        source[s] = -1
    for t in range(8):
        rank = lax.bitwise_and(lax.shift_right_logical(code[t], 2), 3)

        @pl.when((code[t] >= 16) & (lax.bitwise_and(code[t], 3) == g))
        def _():
            source[g * CAP + rank] = t

    for s in range(16):
        own = g == s // CAP

        @pl.when(own)
        def _():
            pltpu.make_async_copy(local.at[jnp.maximum(source[s], 0)], rows.at[s], sem_t.at[s]).start()

        @pl.when(jnp.logical_not(own))
        def _():
            pltpu.make_async_copy(arrived.at[s // CAP, s % CAP], rows.at[s], sem_t.at[s]).start()

    copies = []
    for side, buffers in enumerate((mine, sibling)):
        core = c if side == 0 else 1 - c
        pieces = [buffer.at[k] for buffer in buffers for k in range(2)]
        for n, (piece, chip) in enumerate(zip(pieces, chips_of(y, z, core), strict=True)):
            to = matrix.at[pl.ds(pl.multiple_of(chip * height, height), height), pl.ds(pl.multiple_of(core * half, 128), half)]
            copies.append(pltpu.make_async_copy(piece, to, sem_i.at[side, n]))
    for copy in copies:
        copy.start()

    zero[...] = jnp.zeros_like(zero)
    for s in range(16):
        pltpu.make_async_copy(local.at[0], rows.at[s], sem_t.at[s]).wait()
    count = jnp.int32(0)
    for s in range(16):
        found = jnp.max(jnp.where(jnp.isnan(rows[s, :MARK, :128].astype(jnp.float32)), 0.0, 1.0)) > 0.5
        taken = ((g == s // CAP) & (source[s] >= 0)) | ((g != s // CAP) & found)
        order[s] = 0

        @pl.when(taken)
        def _():
            order[count] = s

        @pl.when(jnp.logical_not(taken))
        def _():
            pltpu.make_async_copy(zero, out.at[s], sem_z.at[s]).start()

        source[s] = taken.astype(jnp.int32)
        count = count + taken.astype(jnp.int32)

    for copy in copies:
        copy.wait()

    pairs = lax.shift_right_logical(count + 1, 1)
    large = jnp.where(pairs <= 4, pairs, lax.shift_right_logical(pairs + 1, 1))

    @pl.loop(0, 2)
    def _(turn):
        start = turn * large * 2
        size = jnp.where(turn == 0, large, pairs - large)
        for group, low in ((4, 1), (6, 3), (8, 4)):

            @pl.when((size >= low) & (size <= group // 2))
            def _():
                tile = lambda j: order[jnp.minimum(start + j, 15)]
                left = jnp.concatenate([rows[tile(j)] for j in range(group)], axis=0)
                for n in range(width // step):
                    right = matrix[n * step : (n + 1) * step, :]
                    acc = lax.dot_general(left, right, (((1,), (1,)), ((), ())), preferred_element_type=jnp.float32)
                    result[pl.ds(start, group), :, n * step : (n + 1) * step] = acc.astype(result.dtype).reshape(group, occ, step)
                for j in range(group):

                    @pl.when((start + j < count) & (j < 2 * size))
                    def _():
                        pltpu.make_async_copy(result.at[start + j], out.at[tile(j)], sem_o.at[start + j]).start()

    for s in range(16):

        @pl.when(s < count)
        def _():
            pltpu.make_async_copy(result.at[s], out.at[order[s]], sem_o.at[s]).wait()

        @pl.when(source[s] == 0)
        def _():
            pltpu.make_async_copy(zero, out.at[s], sem_z.at[s]).wait()


def product(place, code, local, arrived, pieces):
    occ, width = local.shape[1:]
    return pl.pallas_call(
        product_kernel,
        out_shape=jax.ShapeDtypeStruct((16, occ, width), BF16),
        in_specs=[SMEM, SMEM] + [ANY] * (2 + len(pieces)),
        out_specs=ANY,
        scratch_shapes=[
            pltpu.VMEM((16, occ, width), BF16),
            pltpu.VMEM((width, width), BF16),
            pltpu.VMEM((18, occ, width), BF16),
            pltpu.VMEM((occ, width), BF16),
            pltpu.SMEM((16,), jnp.int32),
            pltpu.SMEM((16,), jnp.int32),
            pltpu.SemaphoreType.DMA((16,)),
            pltpu.SemaphoreType.DMA((2, 16)),
            pltpu.SemaphoreType.DMA((16,)),
            pltpu.SemaphoreType.DMA((16,)),
        ],
        compiler_params=pltpu.CompilerParams(vmem_limit_bytes=56 << 20),
        cost_estimate=pl.CostEstimate(flops=2 * 832 * width * width, bytes_accessed=20_000_000, transcendentals=0),
    )(place, code, local, arrived, *pieces)


def index(y, z, c):
    return ((y % Y) * Y + z % Y) * 2 + c


def permutation(move):
    return [(index(y, z, c), index(*move(y, z, c))) for y in range(Y) for z in range(Y) for c in range(2)]


SWAP = permutation(lambda y, z, c: (y, z, 1 - c))


def first(s):
    return permutation(lambda y, z, c: (y + s, z, c) if c == 0 else (y, z + s, c))


def second(s):
    return permutation(lambda y, z, c: (y, z + s, c) if c == 0 else (y + s, z, c))


def send(x, pairs):
    return lax.ppermute(x, "blk", pairs)


def ring(x, s):
    return lax.ppermute(x, "grp", [(g, (g + s) % 4) for g in range(4)])


def rows_of_chip(integrals):
    core = lax.axis_index("blk") % 2
    half = integrals.shape[1] // 2
    sibling = send(integrals, SWAP)
    mine = jnp.where(core == 0, integrals[:, :half], integrals[:, half:])
    its = jnp.where(core == 0, sibling[:, :half], sibling[:, half:])
    return jnp.concatenate([jnp.where(core == 0, mine, its), jnp.where(core == 0, its, mine)], 0)


def gather(own):
    before, behind = send(own, first(1)), send(own, first(-1))
    opposite = send(before, first(1))
    near, wide = jnp.stack([own, before]), jnp.stack([behind, opposite])
    near_up, wide_down = send(near, second(1)), send(wide, second(-1))
    wide_up, near_down = send(wide, second(1)), send(near, second(-1))
    near_far, wide_far = send(near_up, second(1)), send(wide_down, second(-1))
    moved = [near_up, wide_down, wide_up, near_down, near_far, wide_far]
    mine = [near, wide] + moved
    return mine + [send(m, SWAP) for m in mine]


def as_one(owners, f, *args):
    empty = lambda *a: jax.tree.map(lambda x: jnp.zeros(x.shape, x.dtype), jax.eval_shape(f, *a))
    return lax.cond(owners[0, 0] >= 0, f, empty, *args)


def body(t2, t2_shape, owners, integrals):
    g, b = lax.axis_index("grp"), lax.axis_index("blk")
    position = jnp.stack([b // 8, (b // 2) % 4, b % 2, g]).astype(jnp.int32)
    code, out = pack(owners[:, 0], t2_shape[:, 0], t2)
    arrived = lax.all_to_all(out, "grp", split_axis=0, concat_axis=0, tiled=True)
    pieces = as_one(owners, gather, rows_of_chip(integrals))
    return product(position, code, t2, arrived, pieces)


def solution(mesh):
    in_specs = (
        P(("grp", "blk"), None, None),
        P(("grp", "blk"), None),
        P(("grp", "blk"), None),
        P("blk", None),
    )
    out_specs = P(("grp", "blk"), None, None)
    return jax.shard_map(body, mesh=mesh, in_specs=in_specs, out_specs=out_specs, check_vma=False)
```

```python
import functools

import jax
import jax.numpy as jnp
from jax import lax
from jax.experimental import pallas as pl
from jax.experimental.pallas import tpu as pltpu
from jax.sharding import PartitionSpec as P

Y = 4
CAP = 4
MARK = 16
ANY = pl.BlockSpec(memory_space=pl.ANY)
SMEM = pl.BlockSpec(memory_space=pltpu.SMEM)
VMEM = pl.BlockSpec(memory_space=pltpu.VMEM)
BF16 = jnp.bfloat16


def pack_kernel(owners_hbm, shape_hbm, t2, code, out, owners, shape, tiles, mark, sem_s, sem_i, sem_o, sem_m):
    small = [pltpu.make_async_copy(owners_hbm, owners, sem_s.at[0]), pltpu.make_async_copy(shape_hbm, shape, sem_s.at[1])]
    for load in small:
        load.start()
    loads = [pltpu.make_async_copy(t2.at[t], tiles.at[t], sem_i.at[t]) for t in range(8)]
    for load in loads:
        load.start()
    mark[...] = jnp.full(mark.shape, jnp.nan, mark.dtype)
    for load in small:
        load.wait()
    taken = jnp.int32(0)
    for t in range(8):
        rank = 0
        for e in range(t):
            rank = rank + (owners[e] == owners[t]).astype(jnp.int32)
        live = (shape[t] > 0).astype(jnp.int32)
        code[t] = owners[t] + 4 * rank + 16 * live
        taken = taken | lax.shift_left(live, owners[t] * CAP + rank)

    def marks(do):
        for s in range(16):

            @pl.when(lax.bitwise_and(lax.shift_right_logical(taken, s), 1) == 0)
            def _():
                do(pltpu.make_async_copy(mark, out.at[s // CAP, s % CAP, pl.ds(0, MARK), pl.ds(0, 128)], sem_m.at[s]))

    def moves(do):
        for t in range(8):

            @pl.when(code[t] >= 16)
            def _():
                place = out.at[lax.bitwise_and(code[t], 3), lax.bitwise_and(lax.shift_right_logical(code[t], 2), 3)]
                do(loads[t], pltpu.make_async_copy(tiles.at[t], place, sem_o.at[t]))

            if do is start:

                @pl.when(code[t] < 16)
                def _():
                    loads[t].wait()

    def start(load, move):
        load.wait()
        move.start()

    marks(lambda c: c.start())
    moves(start)
    marks(lambda c: c.wait())
    moves(lambda load, move: move.wait())


def pack(owners, shape, t2):
    return pl.pallas_call(
        pack_kernel,
        out_shape=(jax.ShapeDtypeStruct((8,), jnp.int32), jax.ShapeDtypeStruct((4, CAP) + t2.shape[1:], t2.dtype)),
        in_specs=[ANY, ANY, ANY],
        out_specs=(SMEM, ANY),
        scratch_shapes=[
            pltpu.SMEM((8,), jnp.int32),
            pltpu.SMEM((8,), jnp.int32),
            pltpu.VMEM(t2.shape, t2.dtype),
            pltpu.VMEM((MARK, 128), t2.dtype),
            pltpu.SemaphoreType.DMA((2,)),
            pltpu.SemaphoreType.DMA((8,)),
            pltpu.SemaphoreType.DMA((8,)),
            pltpu.SemaphoreType.DMA((16,)),
        ],
        compiler_params=pltpu.CompilerParams(vmem_limit_bytes=56 << 20),
        cost_estimate=pl.CostEstimate(flops=0, bytes_accessed=4_700_000, transcendentals=0),
    )(owners, shape, t2)


def chips_of(y, z, c):
    a, b = jnp.where(c == 0, y, z), jnp.where(c == 0, z, y)

    def chip(da, db):
        aa, bb = lax.bitwise_and(a + da, 3), lax.bitwise_and(b + db, 3)
        return jnp.where(c == 0, aa * Y + bb, bb * Y + aa)

    near = lambda db: [chip(0, db), chip(-1, db)]
    wide = lambda db: [chip(1, db), chip(2, db)]
    return near(0) + wide(0) + near(-1) + wide(1) + wide(-1) + near(1) + near(2) + wide(2)


def product_kernel(code, local, arrived, *refs):
    mine, sibling, refs = refs[:8], refs[8:16], refs[16:]
    out, rows, matrix, result, zero, source, order, sem_t, sem_i, sem_o, sem_z = refs
    g, b = lax.axis_index("grp"), lax.axis_index("blk")
    y, z, c = lax.shift_right_logical(b, 3), lax.bitwise_and(lax.shift_right_logical(b, 1), 3), lax.bitwise_and(b, 1)
    half = matrix.shape[1] // 2
    height = mine[0].shape[1]
    width = matrix.shape[0]
    step, occ = 256, rows.shape[1]

    for s in range(16):
        source[s] = -1
    for t in range(8):
        rank = lax.bitwise_and(lax.shift_right_logical(code[t], 2), 3)

        @pl.when((code[t] >= 16) & (lax.bitwise_and(code[t], 3) == g))
        def _():
            source[g * CAP + rank] = t

    for s in range(16):
        own = g == s // CAP

        @pl.when(own)
        def _():
            pltpu.make_async_copy(local.at[jnp.maximum(source[s], 0)], rows.at[s], sem_t.at[s]).start()

        @pl.when(jnp.logical_not(own))
        def _():
            pltpu.make_async_copy(arrived.at[s // CAP, s % CAP], rows.at[s], sem_t.at[s]).start()

    copies = []
    for side, buffers in enumerate((mine, sibling)):
        core = c if side == 0 else 1 - c
        pieces = [buffer.at[k] for buffer in buffers for k in range(2)]
        for n, (piece, chip) in enumerate(zip(pieces, chips_of(y, z, core), strict=True)):
            to = matrix.at[pl.ds(pl.multiple_of(chip * height, height), height), pl.ds(pl.multiple_of(core * half, 128), half)]
            copies.append(pltpu.make_async_copy(piece, to, sem_i.at[side, n]))
    for copy in copies:
        copy.start()

    zero[...] = jnp.zeros_like(zero)
    for s in range(16):
        pltpu.make_async_copy(local.at[0], rows.at[s], sem_t.at[s]).wait()
    count = jnp.int32(0)
    for s in range(16):
        found = jnp.max(jnp.where(jnp.isnan(rows[s, :MARK, :128].astype(jnp.float32)), 0.0, 1.0)) > 0.5
        taken = ((g == s // CAP) & (source[s] >= 0)) | ((g != s // CAP) & found)
        order[s] = 0

        @pl.when(taken)
        def _():
            order[count] = s

        @pl.when(jnp.logical_not(taken))
        def _():
            pltpu.make_async_copy(zero, out.at[s], sem_z.at[s]).start()

        source[s] = taken.astype(jnp.int32)
        count = count + taken.astype(jnp.int32)

    for copy in copies:
        copy.wait()

    split = (width // step // 2 + 1) * step
    cuts = ((0, split), (split, width - split))

    def one_pass(group, start, end):
        tile = lambda j: order[jnp.minimum(start + j, 15)]
        left = jnp.concatenate([rows[tile(j)] for j in range(group)], axis=0)
        for n in range(width // step):
            right = matrix[n * step : (n + 1) * step, :]
            acc = lax.dot_general(left, right, (((1,), (1,)), ((), ())), preferred_element_type=jnp.float32)
            result[pl.ds(start, group), :, n * step : (n + 1) * step] = acc.astype(result.dtype).reshape(group, occ, step)
            for h, (at, size) in enumerate(cuts):
                if (n + 1) * step == at + size:
                    for j in range(group):

                        @pl.when(start + j < end)
                        def _():
                            cols = pl.ds(at, size)
                            pltpu.make_async_copy(result.at[start + j, :, cols], out.at[tile(j), :, cols], sem_o.at[h, start + j]).start()

    some = jnp.maximum(lax.shift_right_logical(count + 1, 2), 1)

    @pl.loop(0, some)
    def _(turn):
        last = turn == some - 1
        six = last & (count - turn * 4 > 4)

        @pl.when(jnp.logical_not(six))
        def _():
            one_pass(4, turn * 4, count)

        @pl.when(six)
        def _():
            one_pass(6, turn * 4, count)

    for s in range(16):

        @pl.when(s < count)
        def _():
            for h in range(2):
                cols = pl.ds(*cuts[h])
                pltpu.make_async_copy(result.at[s, :, cols], out.at[order[s], :, cols], sem_o.at[h, s]).wait()

        @pl.when(source[s] == 0)
        def _():
            pltpu.make_async_copy(zero, out.at[s], sem_z.at[s]).wait()


def product(code, local, arrived, pieces):
    occ, width = local.shape[1:]
    return pl.pallas_call(
        product_kernel,
        out_shape=jax.ShapeDtypeStruct((16, occ, width), BF16),
        in_specs=[SMEM] + [ANY] * (2 + len(pieces)),
        out_specs=ANY,
        scratch_shapes=[
            pltpu.VMEM((16, occ, width), BF16),
            pltpu.VMEM((width, width), BF16),
            pltpu.VMEM((18, occ, width), BF16),
            pltpu.VMEM((occ, width), BF16),
            pltpu.SMEM((16,), jnp.int32),
            pltpu.SMEM((16,), jnp.int32),
            pltpu.SemaphoreType.DMA((16,)),
            pltpu.SemaphoreType.DMA((2, 16)),
            pltpu.SemaphoreType.DMA((2, 16)),
            pltpu.SemaphoreType.DMA((16,)),
        ],
        compiler_params=pltpu.CompilerParams(vmem_limit_bytes=56 << 20),
        cost_estimate=pl.CostEstimate(flops=2 * 832 * width * width, bytes_accessed=20_000_000, transcendentals=0),
    )(code, local, arrived, *pieces)


def index(y, z, c):
    return ((y % Y) * Y + z % Y) * 2 + c


def permutation(move):
    return [(index(y, z, c), index(*move(y, z, c))) for y in range(Y) for z in range(Y) for c in range(2)]


SWAP = permutation(lambda y, z, c: (y, z, 1 - c))


def first(s):
    return permutation(lambda y, z, c: (y + s, z, c) if c == 0 else (y, z + s, c))


def second(s):
    return permutation(lambda y, z, c: (y, z + s, c) if c == 0 else (y + s, z, c))


def send(x, pairs):
    return lax.ppermute(x, "blk", pairs)


def ring(x, s):
    return lax.ppermute(x, "grp", [(g, (g + s) % 4) for g in range(4)])


def rows_of_chip(integrals):
    core = lax.axis_index("blk") % 2
    half = integrals.shape[1] // 2
    sibling = send(integrals, SWAP)
    mine = jnp.where(core == 0, integrals[:, :half], integrals[:, half:])
    its = jnp.where(core == 0, sibling[:, :half], sibling[:, half:])
    return jnp.concatenate([jnp.where(core == 0, mine, its), jnp.where(core == 0, its, mine)], 0)


def gather(own):
    before, behind = send(own, first(1)), send(own, first(-1))
    opposite = send(before, first(1))
    near, wide = jnp.stack([own, before]), jnp.stack([behind, opposite])
    near_up, wide_down = send(near, second(1)), send(wide, second(-1))
    wide_up, near_down = send(wide, second(1)), send(near, second(-1))
    near_far, wide_far = send(near_up, second(1)), send(wide_down, second(-1))
    moved = [near_up, wide_down, wide_up, near_down, near_far, wide_far]
    mine = [near, wide] + moved
    return mine + [send(m, SWAP) for m in mine]


def as_one(owners, f, *args):
    empty = lambda *a: jax.tree.map(lambda x: jnp.zeros(x.shape, x.dtype), jax.eval_shape(f, *a))
    return lax.cond(owners[0, 0] >= 0, f, empty, *args)


def body(t2, t2_shape, owners, integrals):
    code, out = pack(owners[:, 0], t2_shape[:, 0], t2)
    arrived = lax.all_to_all(out, "grp", split_axis=0, concat_axis=0, tiled=True)
    pieces = as_one(owners, gather, rows_of_chip(integrals))
    return product(code, t2, arrived, pieces)


def solution(mesh):
    in_specs = (
        P(("grp", "blk"), None, None),
        P(("grp", "blk"), None),
        P(("grp", "blk"), None),
        P("blk", None),
    )
    out_specs = P(("grp", "blk"), None, None)
    return jax.shard_map(body, mesh=mesh, in_specs=in_specs, out_specs=out_specs, check_vma=False)
```

```python
import functools

import jax
import jax.numpy as jnp
from jax import lax
from jax.experimental import pallas as pl
from jax.experimental.pallas import tpu as pltpu
from jax.sharding import PartitionSpec as P

Y = 4
CAP = 4
MARK = 16
ANY = pl.BlockSpec(memory_space=pl.ANY)
SMEM = pl.BlockSpec(memory_space=pltpu.SMEM)
VMEM = pl.BlockSpec(memory_space=pltpu.VMEM)
BF16 = jnp.bfloat16


def pack_kernel(owners_hbm, shape_hbm, t2, code, out, owners, shape, tiles, mark, sem_s, sem_i, sem_o, sem_m):
    small = [pltpu.make_async_copy(owners_hbm, owners, sem_s.at[0]), pltpu.make_async_copy(shape_hbm, shape, sem_s.at[1])]
    for load in small:
        load.start()
    loads = [pltpu.make_async_copy(t2.at[t], tiles.at[t], sem_i.at[t]) for t in range(8)]
    for load in loads:
        load.start()
    mark[...] = jnp.full(mark.shape, jnp.nan, mark.dtype)
    for load in small:
        load.wait()
    taken = jnp.int32(0)
    for t in range(8):
        rank = 0
        for e in range(t):
            rank = rank + (owners[e] == owners[t]).astype(jnp.int32)
        live = (shape[t] > 0).astype(jnp.int32)
        code[t] = owners[t] + 4 * rank + 16 * live
        taken = taken | lax.shift_left(live, owners[t] * CAP + rank)

    def marks(do):
        for s in range(16):

            @pl.when(lax.bitwise_and(lax.shift_right_logical(taken, s), 1) == 0)
            def _():
                do(pltpu.make_async_copy(mark, out.at[s // CAP, s % CAP, pl.ds(0, MARK), pl.ds(0, 128)], sem_m.at[s]))

    def moves(do):
        for t in range(8):

            @pl.when(code[t] >= 16)
            def _():
                place = out.at[lax.bitwise_and(code[t], 3), lax.bitwise_and(lax.shift_right_logical(code[t], 2), 3)]
                do(loads[t], pltpu.make_async_copy(tiles.at[t], place, sem_o.at[t]))

            if do is start:

                @pl.when(code[t] < 16)
                def _():
                    loads[t].wait()

    def start(load, move):
        load.wait()
        move.start()

    marks(lambda c: c.start())
    moves(start)
    marks(lambda c: c.wait())
    moves(lambda load, move: move.wait())


def pack(owners, shape, t2):
    return pl.pallas_call(
        pack_kernel,
        out_shape=(jax.ShapeDtypeStruct((8,), jnp.int32), jax.ShapeDtypeStruct((4, CAP) + t2.shape[1:], t2.dtype)),
        in_specs=[ANY, ANY, ANY],
        out_specs=(SMEM, ANY),
        scratch_shapes=[
            pltpu.SMEM((8,), jnp.int32),
            pltpu.SMEM((8,), jnp.int32),
            pltpu.VMEM(t2.shape, t2.dtype),
            pltpu.VMEM((MARK, 128), t2.dtype),
            pltpu.SemaphoreType.DMA((2,)),
            pltpu.SemaphoreType.DMA((8,)),
            pltpu.SemaphoreType.DMA((8,)),
            pltpu.SemaphoreType.DMA((16,)),
        ],
        compiler_params=pltpu.CompilerParams(vmem_limit_bytes=56 << 20),
        cost_estimate=pl.CostEstimate(flops=0, bytes_accessed=4_700_000, transcendentals=0),
    )(owners, shape, t2)


def chips_of(y, z, c):
    a, b = jnp.where(c == 0, y, z), jnp.where(c == 0, z, y)

    def chip(da, db):
        aa, bb = lax.bitwise_and(a + da, 3), lax.bitwise_and(b + db, 3)
        return jnp.where(c == 0, aa * Y + bb, bb * Y + aa)

    near = lambda db: [chip(0, db), chip(-1, db)]
    wide = lambda db: [chip(1, db), chip(2, db)]
    return near(0) + wide(0) + near(-1) + wide(1) + wide(-1) + near(1) + near(2) + wide(2)


def product_kernel(code, local, arrived, *refs):
    mine, sibling, refs = refs[:8], refs[8:16], refs[16:]
    out, rows, matrix, result, zero, source, order, sem_t, sem_i, sem_o, sem_z = refs
    g, b = lax.axis_index("grp"), lax.axis_index("blk")
    y, z, c = lax.shift_right_logical(b, 3), lax.bitwise_and(lax.shift_right_logical(b, 1), 3), lax.bitwise_and(b, 1)
    half = matrix.shape[1] // 2
    height = mine[0].shape[1]
    width = matrix.shape[0]
    step, occ = 256, rows.shape[1]

    for s in range(16):
        source[s] = -1
    for t in range(8):
        rank = lax.bitwise_and(lax.shift_right_logical(code[t], 2), 3)

        @pl.when((code[t] >= 16) & (lax.bitwise_and(code[t], 3) == g))
        def _():
            source[g * CAP + rank] = t

    for s in range(16):
        own = g == s // CAP

        @pl.when(own)
        def _():
            pltpu.make_async_copy(local.at[jnp.maximum(source[s], 0)], rows.at[s], sem_t.at[s]).start()

        @pl.when(jnp.logical_not(own))
        def _():
            pltpu.make_async_copy(arrived.at[s // CAP, s % CAP], rows.at[s], sem_t.at[s]).start()

    copies = []
    for side, buffers in enumerate((mine, sibling)):
        core = c if side == 0 else 1 - c
        pieces = [buffer.at[k] for buffer in buffers for k in range(2)]
        for n, (piece, chip) in enumerate(zip(pieces, chips_of(y, z, core), strict=True)):
            to = matrix.at[pl.ds(pl.multiple_of(chip * height, height), height), pl.ds(pl.multiple_of(core * half, 128), half)]
            copies.append(pltpu.make_async_copy(piece, to, sem_i.at[side, n]))
    for copy in copies:
        copy.start()

    zero[...] = jnp.zeros_like(zero)
    for s in range(16):
        pltpu.make_async_copy(local.at[0], rows.at[s], sem_t.at[s]).wait()
    count = jnp.int32(0)
    for s in range(16):
        found = jnp.max(jnp.where(jnp.isnan(rows[s, :MARK, :128].astype(jnp.float32)), 0.0, 1.0)) > 0.5
        taken = ((g == s // CAP) & (source[s] >= 0)) | ((g != s // CAP) & found)
        order[s] = 0

        @pl.when(taken)
        def _():
            order[count] = s

        @pl.when(jnp.logical_not(taken))
        def _():
            pltpu.make_async_copy(zero, out.at[s], sem_z.at[s]).start()

        source[s] = taken.astype(jnp.int32)
        count = count + taken.astype(jnp.int32)

    for copy in copies:
        copy.wait()

    split = (width // step // 2 + 1) * step
    cuts = ((0, split), (split, width - split))

    def one_pass(group, start, end):
        tile = lambda j: order[jnp.minimum(start + j, 15)]
        left = jnp.concatenate([rows[tile(j)] for j in range(group)], axis=0)
        for n in range(width // step):
            right = matrix[n * step : (n + 1) * step, :]
            acc = lax.dot_general(left, right, (((1,), (1,)), ((), ())), preferred_element_type=jnp.float32)
            result[pl.ds(start, group), :, n * step : (n + 1) * step] = acc.astype(result.dtype).reshape(group, occ, step)
            for h, (at, size) in enumerate(cuts):
                if (n + 1) * step == at + size:
                    for j in range(group):

                        @pl.when(start + j < end)
                        def _():
                            cols = pl.ds(at, size)
                            pltpu.make_async_copy(result.at[start + j, :, cols], out.at[tile(j), :, cols], sem_o.at[h, start + j]).start()

    some = jnp.maximum(lax.shift_right_logical(count + 1, 2), 1)

    @pl.loop(0, some)
    def _(turn):
        last = turn == some - 1
        six = last & (count - turn * 4 > 4)

        @pl.when(jnp.logical_not(six))
        def _():
            one_pass(4, turn * 4, count)

        @pl.when(six)
        def _():
            one_pass(6, turn * 4, count)

    for s in range(16):

        @pl.when(s < count)
        def _():
            for h in range(2):
                cols = pl.ds(*cuts[h])
                pltpu.make_async_copy(result.at[s, :, cols], out.at[order[s], :, cols], sem_o.at[h, s]).wait()

        @pl.when(source[s] == 0)
        def _():
            pltpu.make_async_copy(zero, out.at[s], sem_z.at[s]).wait()


def product(code, local, arrived, pieces):
    occ, width = local.shape[1:]
    return pl.pallas_call(
        product_kernel,
        out_shape=jax.ShapeDtypeStruct((16, occ, width), BF16),
        in_specs=[SMEM] + [ANY] * (2 + len(pieces)),
        out_specs=ANY,
        scratch_shapes=[
            pltpu.VMEM((16, occ, width), BF16),
            pltpu.VMEM((width, width), BF16),
            pltpu.VMEM((18, occ, width), BF16),
            pltpu.VMEM((occ, width), BF16),
            pltpu.SMEM((16,), jnp.int32),
            pltpu.SMEM((16,), jnp.int32),
            pltpu.SemaphoreType.DMA((16,)),
            pltpu.SemaphoreType.DMA((2, 16)),
            pltpu.SemaphoreType.DMA((2, 16)),
            pltpu.SemaphoreType.DMA((16,)),
        ],
        compiler_params=pltpu.CompilerParams(vmem_limit_bytes=56 << 20),
        cost_estimate=pl.CostEstimate(flops=2 * 832 * width * width, bytes_accessed=20_000_000, transcendentals=0),
    )(code, local, arrived, *pieces)


def index(y, z, c):
    return ((y % Y) * Y + z % Y) * 2 + c


def permutation(move):
    return [(index(y, z, c), index(*move(y, z, c))) for y in range(Y) for z in range(Y) for c in range(2)]


SWAP = permutation(lambda y, z, c: (y, z, 1 - c))


def first(s):
    return permutation(lambda y, z, c: (y + s, z, c) if c == 0 else (y, z + s, c))


def second(s):
    return permutation(lambda y, z, c: (y, z + s, c) if c == 0 else (y + s, z, c))


def send(x, pairs):
    return lax.ppermute(x, "blk", pairs)


def ring(x, s):
    return lax.ppermute(x, "grp", [(g, (g + s) % 4) for g in range(4)])


def rows_of_chip(integrals):
    core = lax.axis_index("blk") % 2
    half = integrals.shape[1] // 2
    sibling = send(integrals, SWAP)
    mine = jnp.where(core == 0, integrals[:, :half], integrals[:, half:])
    its = jnp.where(core == 0, sibling[:, :half], sibling[:, half:])
    return jnp.concatenate([jnp.where(core == 0, mine, its), jnp.where(core == 0, its, mine)], 0)


def gather(own):
    before, behind = send(own, first(1)), send(own, first(-1))
    opposite = send(before, first(1))
    near, wide = jnp.stack([own, before]), jnp.stack([behind, opposite])
    near_up, wide_down = send(near, second(1)), send(wide, second(-1))
    wide_up, near_down = send(wide, second(1)), send(near, second(-1))
    near_far, wide_far = send(near_up, second(1)), send(wide_down, second(-1))
    moved = [near_up, wide_down, wide_up, near_down, near_far, wide_far]
    mine = [near, wide] + moved
    return mine + [send(m, SWAP) for m in mine]


def body(t2, t2_shape, owners, integrals):
    code, out = pack(owners[:, 0], t2_shape[:, 0], t2)
    arrived = lax.all_to_all(out, "grp", split_axis=0, concat_axis=0, tiled=True)
    pieces = gather(rows_of_chip(integrals))
    return product(code, t2, arrived, pieces)


def solution(mesh):
    in_specs = (
        P(("grp", "blk"), None, None),
        P(("grp", "blk"), None),
        P(("grp", "blk"), None),
        P("blk", None),
    )
    out_specs = P(("grp", "blk"), None, None)
    return jax.shard_map(body, mesh=mesh, in_specs=in_specs, out_specs=out_specs, check_vma=False)
```

```python
import functools

import jax
import jax.numpy as jnp
from jax import lax
from jax.experimental import pallas as pl
from jax.experimental.pallas import tpu as pltpu
from jax.sharding import PartitionSpec as P

Y = 4
CAP = 4
MARK = 16
ANY = pl.BlockSpec(memory_space=pl.ANY)
SMEM = pl.BlockSpec(memory_space=pltpu.SMEM)
VMEM = pl.BlockSpec(memory_space=pltpu.VMEM)
BF16 = jnp.bfloat16


def pack_kernel(owners_hbm, shape_hbm, t2, code, out, owners, shape, tiles, mark, sem_s, sem_i, sem_o, sem_m):
    small = [pltpu.make_async_copy(owners_hbm, owners, sem_s.at[0]), pltpu.make_async_copy(shape_hbm, shape, sem_s.at[1])]
    for load in small:
        load.start()
    loads = [pltpu.make_async_copy(t2.at[t], tiles.at[t], sem_i.at[t]) for t in range(8)]
    for load in loads:
        load.start()
    mark[...] = jnp.full(mark.shape, jnp.nan, mark.dtype)
    for load in small:
        load.wait()
    taken = jnp.int32(0)
    for t in range(8):
        rank = 0
        for e in range(t):
            rank = rank + (owners[e] == owners[t]).astype(jnp.int32)
        live = (shape[t] > 0).astype(jnp.int32)
        code[t] = owners[t] + 4 * rank + 16 * live
        taken = taken | lax.shift_left(live, owners[t] * CAP + rank)

    def marks(do):
        for s in range(16):

            @pl.when(lax.bitwise_and(lax.shift_right_logical(taken, s), 1) == 0)
            def _():
                do(pltpu.make_async_copy(mark, out.at[s // CAP, s % CAP, pl.ds(0, MARK), pl.ds(0, 128)], sem_m.at[s]))

    def moves(do):
        for t in range(8):

            @pl.when(code[t] >= 16)
            def _():
                place = out.at[lax.bitwise_and(code[t], 3), lax.bitwise_and(lax.shift_right_logical(code[t], 2), 3)]
                do(loads[t], pltpu.make_async_copy(tiles.at[t], place, sem_o.at[t]))

            if do is start:

                @pl.when(code[t] < 16)
                def _():
                    loads[t].wait()

    def start(load, move):
        load.wait()
        move.start()

    marks(lambda c: c.start())
    moves(start)
    marks(lambda c: c.wait())
    moves(lambda load, move: move.wait())


def pack(owners, shape, t2):
    return pl.pallas_call(
        pack_kernel,
        out_shape=(jax.ShapeDtypeStruct((8,), jnp.int32), jax.ShapeDtypeStruct((4, CAP) + t2.shape[1:], t2.dtype)),
        in_specs=[ANY, ANY, ANY],
        out_specs=(SMEM, ANY),
        scratch_shapes=[
            pltpu.SMEM((8,), jnp.int32),
            pltpu.SMEM((8,), jnp.int32),
            pltpu.VMEM(t2.shape, t2.dtype),
            pltpu.VMEM((MARK, 128), t2.dtype),
            pltpu.SemaphoreType.DMA((2,)),
            pltpu.SemaphoreType.DMA((8,)),
            pltpu.SemaphoreType.DMA((8,)),
            pltpu.SemaphoreType.DMA((16,)),
        ],
        compiler_params=pltpu.CompilerParams(vmem_limit_bytes=56 << 20),
        cost_estimate=pl.CostEstimate(flops=0, bytes_accessed=4_700_000, transcendentals=0),
    )(owners, shape, t2)


def chips_of(y, z, c):
    a, b = jnp.where(c == 0, y, z), jnp.where(c == 0, z, y)

    def chip(da, db):
        aa, bb = lax.bitwise_and(a + da, 3), lax.bitwise_and(b + db, 3)
        return jnp.where(c == 0, aa * Y + bb, bb * Y + aa)

    near = lambda db: [chip(0, db), chip(-1, db)]
    wide = lambda db: [chip(1, db), chip(2, db)]
    return near(0) + wide(0) + near(-1) + wide(1) + wide(-1) + near(1) + near(2) + wide(2)


def product_kernel(code, local, arrived, *refs):
    mine, sibling, refs = refs[:8], refs[8:16], refs[16:]
    out, rows, matrix, result, zero, source, order, sem_t, sem_i, sem_o, sem_z = refs
    g, b = lax.axis_index("grp"), lax.axis_index("blk")
    y, z, c = lax.shift_right_logical(b, 3), lax.bitwise_and(lax.shift_right_logical(b, 1), 3), lax.bitwise_and(b, 1)
    half = matrix.shape[1] // 2
    height = mine[0].shape[1]
    width = matrix.shape[0]
    step, occ = 256, rows.shape[1]

    for s in range(16):
        source[s] = -1
    for t in range(8):
        rank = lax.bitwise_and(lax.shift_right_logical(code[t], 2), 3)

        @pl.when((code[t] >= 16) & (lax.bitwise_and(code[t], 3) == g))
        def _():
            source[g * CAP + rank] = t

    for s in range(16):
        own = g == s // CAP

        @pl.when(own)
        def _():
            pltpu.make_async_copy(local.at[jnp.maximum(source[s], 0)], rows.at[s], sem_t.at[s]).start()

        @pl.when(jnp.logical_not(own))
        def _():
            pltpu.make_async_copy(arrived.at[s // CAP, s % CAP], rows.at[s], sem_t.at[s]).start()

    copies = []
    for side, buffers in enumerate((mine, sibling)):
        core = c if side == 0 else 1 - c
        pieces = [buffer.at[k] for buffer in buffers for k in range(2)]
        for n, (piece, chip) in enumerate(zip(pieces, chips_of(y, z, core), strict=True)):
            to = matrix.at[pl.ds(pl.multiple_of(chip * height, height), height), pl.ds(pl.multiple_of(core * half, 128), half)]
            copies.append(pltpu.make_async_copy(piece, to, sem_i.at[side, n]))
    for copy in copies:
        copy.start()

    zero[...] = jnp.zeros_like(zero)
    for s in range(16):
        pltpu.make_async_copy(local.at[0], rows.at[s], sem_t.at[s]).wait()
    count = jnp.int32(0)
    for s in range(16):
        found = jnp.max(jnp.where(jnp.isnan(rows[s, :MARK, :128].astype(jnp.float32)), 0.0, 1.0)) > 0.5
        taken = ((g == s // CAP) & (source[s] >= 0)) | ((g != s // CAP) & found)
        order[s] = 0

        @pl.when(taken)
        def _():
            order[count] = s

        source[s] = taken.astype(jnp.int32)
        count = count + taken.astype(jnp.int32)

    for copy in copies:
        copy.wait()
    for s in range(16):

        @pl.when(source[s] == 0)
        def _():
            pltpu.make_async_copy(zero, out.at[s], sem_z.at[s]).start()

    split = (width // step // 2 + 1) * step
    cuts = ((0, split), (split, width - split))

    def one_pass(group, start, end):
        tile = lambda j: order[jnp.minimum(start + j, 15)]
        left = jnp.concatenate([rows[tile(j)] for j in range(group)], axis=0)
        for n in range(width // step):
            right = matrix[n * step : (n + 1) * step, :]
            acc = lax.dot_general(left, right, (((1,), (1,)), ((), ())), preferred_element_type=jnp.float32)
            result[pl.ds(start, group), :, n * step : (n + 1) * step] = acc.astype(result.dtype).reshape(group, occ, step)
            for h, (at, size) in enumerate(cuts):
                if (n + 1) * step == at + size:
                    for j in range(group):

                        @pl.when(start + j < end)
                        def _():
                            cols = pl.ds(at, size)
                            pltpu.make_async_copy(result.at[start + j, :, cols], out.at[tile(j), :, cols], sem_o.at[h, start + j]).start()

    some = jnp.maximum(lax.shift_right_logical(count + 1, 2), 1)

    @pl.loop(0, some)
    def _(turn):
        last = turn == some - 1
        six = last & (count - turn * 4 > 4)

        @pl.when(jnp.logical_not(six))
        def _():
            one_pass(4, turn * 4, count)

        @pl.when(six)
        def _():
            one_pass(6, turn * 4, count)

    for s in range(16):

        @pl.when(s < count)
        def _():
            for h in range(2):
                cols = pl.ds(*cuts[h])
                pltpu.make_async_copy(result.at[s, :, cols], out.at[order[s], :, cols], sem_o.at[h, s]).wait()

        @pl.when(source[s] == 0)
        def _():
            pltpu.make_async_copy(zero, out.at[s], sem_z.at[s]).wait()


def product(code, local, arrived, pieces):
    occ, width = local.shape[1:]
    return pl.pallas_call(
        product_kernel,
        out_shape=jax.ShapeDtypeStruct((16, occ, width), BF16),
        in_specs=[SMEM] + [ANY] * (2 + len(pieces)),
        out_specs=ANY,
        scratch_shapes=[
            pltpu.VMEM((16, occ, width), BF16),
            pltpu.VMEM((width, width), BF16),
            pltpu.VMEM((18, occ, width), BF16),
            pltpu.VMEM((occ, width), BF16),
            pltpu.SMEM((16,), jnp.int32),
            pltpu.SMEM((16,), jnp.int32),
            pltpu.SemaphoreType.DMA((16,)),
            pltpu.SemaphoreType.DMA((2, 16)),
            pltpu.SemaphoreType.DMA((2, 16)),
            pltpu.SemaphoreType.DMA((16,)),
        ],
        compiler_params=pltpu.CompilerParams(vmem_limit_bytes=56 << 20),
        cost_estimate=pl.CostEstimate(flops=2 * 832 * width * width, bytes_accessed=20_000_000, transcendentals=0),
    )(code, local, arrived, *pieces)


def index(y, z, c):
    return ((y % Y) * Y + z % Y) * 2 + c


def permutation(move):
    return [(index(y, z, c), index(*move(y, z, c))) for y in range(Y) for z in range(Y) for c in range(2)]


SWAP = permutation(lambda y, z, c: (y, z, 1 - c))


def first(s):
    return permutation(lambda y, z, c: (y + s, z, c) if c == 0 else (y, z + s, c))


def second(s):
    return permutation(lambda y, z, c: (y, z + s, c) if c == 0 else (y + s, z, c))


def send(x, pairs):
    return lax.ppermute(x, "blk", pairs)


def ring(x, s):
    return lax.ppermute(x, "grp", [(g, (g + s) % 4) for g in range(4)])


def rows_of_chip(integrals):
    core = lax.axis_index("blk") % 2
    half = integrals.shape[1] // 2
    sibling = send(integrals, SWAP)
    mine = jnp.where(core == 0, integrals[:, :half], integrals[:, half:])
    its = jnp.where(core == 0, sibling[:, :half], sibling[:, half:])
    return jnp.concatenate([jnp.where(core == 0, mine, its), jnp.where(core == 0, its, mine)], 0)


def gather(own):
    before, behind = send(own, first(1)), send(own, first(-1))
    opposite = send(before, first(1))
    near, wide = jnp.stack([own, before]), jnp.stack([behind, opposite])
    near_up, wide_down = send(near, second(1)), send(wide, second(-1))
    wide_up, near_down = send(wide, second(1)), send(near, second(-1))
    near_far, wide_far = send(near_up, second(1)), send(wide_down, second(-1))
    moved = [near_up, wide_down, wide_up, near_down, near_far, wide_far]
    mine = [near, wide] + moved
    return mine + [send(m, SWAP) for m in mine]


def as_one(owners, f, *args):
    empty = lambda *a: jax.tree.map(lambda x: jnp.zeros(x.shape, x.dtype), jax.eval_shape(f, *a))
    return lax.cond(owners[0, 0] >= 0, f, empty, *args)


def body(t2, t2_shape, owners, integrals):
    code, out = pack(owners[:, 0], t2_shape[:, 0], t2)
    arrived = lax.all_to_all(out, "grp", split_axis=0, concat_axis=0, tiled=True)
    pieces = as_one(owners, gather, rows_of_chip(integrals))
    return product(code, t2, arrived, pieces)


def solution(mesh):
    in_specs = (
        P(("grp", "blk"), None, None),
        P(("grp", "blk"), None),
        P(("grp", "blk"), None),
        P("blk", None),
    )
    out_specs = P(("grp", "blk"), None, None)
    return jax.shard_map(body, mesh=mesh, in_specs=in_specs, out_specs=out_specs, check_vma=False)
```
